256 devices in a mesh: rep: 32 (over y, x, core), head: 8 (over z).
Axes of the slice: x: 4, y: 4, z: 8, core: 2. Of those that a mesh axis runs over, the one named last changes fastest.
Arguments:
- tokens: bfloat16 [16384, 2048], P(('rep', 'head')), may hold values from -6 to 6
- parent_state: bfloat16 [128, 32, 128, 128], P('rep', 'head'), may hold values from -6 to 6
- parent_index: int32 [256], replicated, may hold values from 0 to 127, as said below
- w_qkvz: bfloat16 [2048, 12288], P(None, 'head'), may hold values from -0.125 to 0.125
- w_ba: bfloat16 [2048, 64], P(None, 'head'), may hold values from -0.125 to 0.125
- decay_rate: float32 [32], P('head'), may hold values from 0.01 to 0.12
- norm_gain: float32 [128], replicated, may hold values from 0.1 to 1.9
- w_out: bfloat16 [4096, 2048], P('head'), may hold values from -0.09375 to 0.09375
Outputs:
- mixed: bfloat16 [16384, 2048], P(('rep', 'head'))
The draws below stay inside these ranges and needn't reach their ends.
Inputs may be any that keep to these rules, and one draw needn't show every extreme that they name: `parent_index`: children c in [r * 8, (r+1) * 8) form rep index r. For any two rep indices r and s, the children of r name at most 2 distinct parents among those of s (parents s * 4 to (s+1) * 4 - 1), and every r reaches 2 for some s.
All inputs are finite; a program needn't handle non-finite values.
Results may differ from the reference program's by a relative error of at most 0.017.
Values may be sent and summed in bfloat16 or wider, within the bound.
No kernel may reach another device: no remote copies, remote signals or barrier semaphores. Data moves between devices by JAX's collectives and lax.ppermute only.
A program may use at most 128 MiB of HBM per device.

```python
import math
import jax
import jax.numpy as jnp
from jax import lax

D = 2048
VHEADS = 32
KHEADS = 16
DK = 128
DV = 128
SPAN = 64
CHILD_DEV = 8
PAR_DEV = 4
PARENTS = 128
TOKENS = 16384
N_REP = 32
N_HEAD = 8


def draw_parent_index(key, part):
    key = jax.random.fold_in(key, 17)
    key_anchor, key_base, key_toggle = jax.random.split(key, 3)
    column = jnp.arange(CHILD_DEV)[None, :]
    rotation = jax.random.randint(key_anchor, (N_REP, 1), 0, N_REP)
    target_rep = jnp.arange(N_REP)[:, None]
    anchor = (target_rep + rotation + jnp.maximum(column - 1, 0)) % N_REP
    offset_base = jax.random.randint(key_base, (N_REP, N_REP), 0, PAR_DEV)
    toggle = jax.random.randint(key_toggle, (N_REP, CHILD_DEV), 0, 2)
    toggle = jnp.where(column == 0, 0, jnp.where(column == 1, 1, toggle))
    target = jnp.broadcast_to(target_rep, (N_REP, CHILD_DEV))
    within = (offset_base[target, anchor] + toggle) % PAR_DEV
    return (anchor * PAR_DEV + within).reshape(-1).astype(jnp.int32)


def levels(key, shape, cuts, smallest, largest):
    def one(axis_at, shards_of):
        draws = jax.random.uniform(jax.random.fold_in(jax.random.fold_in(key, 6), axis_at), (shards_of,), jnp.float32, smallest / len(cuts), largest / len(cuts))
        return jnp.repeat(jnp.exp(draws), shape[axis_at] // shards_of).reshape((-1,) + (1,) * (len(shape) - axis_at - 1))

    loudness = one(*cuts[0])
    for cut in cuts[1:]:
        loudness = loudness * one(*cut)
    return loudness


def scatter_about(own_key, extent, spread, most, cuts=(), held_as=jnp.bfloat16):
    array = spread * jax.random.normal(own_key, extent, jnp.float32)
    if cuts:
        array = array * levels(own_key, extent, cuts, -0.22, 0.18)
    return jnp.clip(array, -most, most).astype(held_as)


def setup_inputs(seed: int = 0) -> dict:
    arg_keys = jax.random.split(jax.random.key(seed), 9)
    tokens = scatter_about(arg_keys[0], (TOKENS, D), 1.0, 6.0, ((0, 256),))
    parent_state = scatter_about(arg_keys[1], (PARENTS, VHEADS, DK, DV), 1.0, 6.0, ((0, 32), (1, 8)))
    parent_index = draw_parent_index(jax.random.fold_in(arg_keys[8], 71), 0)
    w_qkvz = scatter_about(arg_keys[3], (D, KHEADS * (2 * DK + 4 * DV)), D ** -0.5, 0.125, ((1, 8),))
    w_ba = scatter_about(arg_keys[4], (D, KHEADS * 4), D ** -0.5, 0.125, ((1, 8),))
    decay_rate = jnp.clip(jnp.exp(math.log(0.12) - 2.4849066 * jax.random.uniform(arg_keys[5], (VHEADS,), jnp.float32) ** levels(arg_keys[5], (VHEADS,), ((0, 8),), -0.2, 0.2)), 0.01, 0.12)
    norm_gain = jnp.clip(1.0 + 0.18 * jax.random.normal(arg_keys[6], (DV,), jnp.float32), 0.1, 1.9)
    w_out = scatter_about(arg_keys[7], (VHEADS * DV, D), (VHEADS * DV) ** -0.5, 0.09375, ((0, 8),))
    return dict(tokens=tokens, parent_state=parent_state, parent_index=parent_index, w_qkvz=w_qkvz, w_ba=w_ba, decay_rate=decay_rate, norm_gain=norm_gain, w_out=w_out)


def split_heads(projected, key_heads):
    row_count = projected.shape[0]
    group_ratio = VHEADS // KHEADS
    block = 2 * DK + 2 * group_ratio * DV
    main_width = key_heads * block
    main = projected[:, :main_width].reshape(row_count, key_heads, block)
    queries = main[:, :, :DK]
    keyvecs = main[:, :, DK:2 * DK]
    values_h = main[:, :, 2 * DK:2 * DK + group_ratio * DV].reshape(row_count, key_heads * group_ratio, DV)
    out_gate = main[:, :, 2 * DK + group_ratio * DV:].reshape(row_count, key_heads * group_ratio, DV)
    gates_raw = projected[:, main_width:].reshape(row_count, key_heads, 2 * group_ratio)
    strength_in = gates_raw[:, :, :group_ratio].reshape(row_count, key_heads * group_ratio)
    decay_in = gates_raw[:, :, group_ratio:].reshape(row_count, key_heads * group_ratio)
    return (queries, keyvecs, values_h, out_gate, strength_in, decay_in)

def delta_layer(projected, states, decay_rate, norm_gain, key_heads):
    hp = lax.Precision.HIGHEST
    children = states.shape[0]
    group_ratio = VHEADS // KHEADS
    queries, keyvecs, values_h, out_gate, strength_in, decay_in = split_heads(projected, key_heads)
    queries = queries * lax.rsqrt(lax.optimization_barrier(jnp.sum(queries * queries, axis=-1, keepdims=True)) + 1e-06) * DK ** (-0.5)
    keyvecs = keyvecs * lax.rsqrt(lax.optimization_barrier(jnp.sum(keyvecs * keyvecs, axis=-1, keepdims=True)) + 1e-06)
    queries = jnp.repeat(queries, group_ratio, axis=1).reshape(children, SPAN, -1, DK)
    keyvecs = jnp.repeat(keyvecs, group_ratio, axis=1).reshape(children, SPAN, -1, DK)
    values_h = values_h.reshape(children, SPAN, -1, DV)
    out_gate = out_gate.reshape(children, SPAN, -1, DV)
    strength = jax.nn.sigmoid(strength_in).reshape(children, SPAN, -1)
    log_decay = -decay_rate[None, :] * jax.nn.softplus(decay_in)
    cumulative = jnp.cumsum(log_decay.reshape(children, SPAN, -1), axis=1)
    cumul_t = jnp.transpose(cumulative, (0, 2, 1))
    strength_t = jnp.transpose(strength, (0, 2, 1))
    index_i = jnp.arange(SPAN)[:, None]
    index_j = jnp.arange(SPAN)[None, :]
    on_or_below = index_i >= index_j
    below = index_i > index_j
    decay_gap = cumul_t[..., :, None] - cumul_t[..., None, :]
    decay_mat = jnp.where(on_or_below, jnp.exp(jnp.where(on_or_below, decay_gap, 0.0)), 0.0)
    key_gram = jnp.einsum('nihd,njhd->nhij', keyvecs, keyvecs, precision=hp)
    coupling = jnp.where(below, strength_t[..., :, None] * decay_mat * key_gram, 0.0)
    identity_mat = jnp.eye(SPAN, dtype=jnp.float32)
    system = identity_mat + coupling
    keys_t = jnp.transpose(keyvecs, (0, 2, 1, 3))
    queries_t = jnp.transpose(queries, (0, 2, 1, 3))
    values_t = jnp.transpose(values_h, (0, 2, 1, 3))
    targets = jnp.concatenate([(strength_t * jnp.exp(cumul_t))[..., None] * keys_t, strength_t[..., None] * values_t], axis=-1)
    solved = lax.linalg.triangular_solve(system, targets, left_side=True, lower=True, unit_diagonal=True)
    key_part = solved[..., :DK]
    value_part = solved[..., DK:]
    corrected = value_part - jnp.einsum('nhcd,nhde->nhce', key_part, states, precision=hp)
    scores = jnp.einsum('nhid,nhjd->nhij', queries_t, keys_t, precision=hp) * decay_mat
    result = jnp.einsum('nhcd,nhde->nhce', jnp.exp(cumul_t)[..., None] * queries_t, states, precision=hp)
    result = result + jnp.einsum('nhij,nhje->nhie', scores, corrected, precision=hp)
    result = jnp.transpose(result, (0, 2, 1, 3))
    normed = result * lax.rsqrt(lax.optimization_barrier(jnp.mean(result * result, axis=-1, keepdims=True)) + 1e-06)
    gated = normed * norm_gain * jax.nn.silu(out_gate)
    return gated.reshape(children * SPAN, -1).astype(jnp.bfloat16)

def reference(tokens, parent_state, parent_index, w_qkvz, w_ba, decay_rate, norm_gain, w_out):
    group_width = VHEADS // N_HEAD * DV

    def one_block(inputs):
        block_tokens, block_parents = inputs
        projected = jnp.concatenate([jnp.dot(block_tokens.astype(jnp.float32), w_qkvz.astype(jnp.float32), preferred_element_type=jnp.float32), jnp.dot(block_tokens.astype(jnp.float32), w_ba.astype(jnp.float32), preferred_element_type=jnp.float32)], axis=1)
        states = parent_state[block_parents].astype(jnp.float32)
        gated = delta_layer(projected, states, decay_rate, norm_gain, KHEADS)
        total = jnp.zeros((gated.shape[0], D), jnp.float32)
        for group in range(N_HEAD):
            partial_term = jnp.dot(gated[:, group * group_width:(group + 1) * group_width].astype(jnp.float32), w_out[group * group_width:(group + 1) * group_width].astype(jnp.float32), preferred_element_type=jnp.float32).astype(jnp.bfloat16)
            partial_term = lax.optimization_barrier(partial_term)
            total = total + partial_term.astype(jnp.float32)
        return total.astype(jnp.bfloat16)
    blocks = lax.map(one_block, (tokens.reshape(N_REP, CHILD_DEV * SPAN, D), parent_index.reshape(N_REP, CHILD_DEV)))
    return blocks.reshape(TOKENS, D)
```

```python
import functools
import jax, jax.numpy as jnp
from jax import lax
from jax.experimental import pallas as pl
from jax.experimental.pallas import tpu as pltpu
DK=128; SPAN=64
BF=jnp.bfloat16; F32=jnp.float32

def split2(a):
    hi = a.astype(BF)
    return hi, (a - hi.astype(F32)).astype(BF)

def dot_nn(a, b):
    return lax.dot_general(a, b, (((1,), (0,)), ((), ())), preferred_element_type=F32)

def dot_nt(a, b):
    return lax.dot_general(a, b, (((1,), (1,)), ((), ())), preferred_element_type=F32)

def mm3(a, b):
    ah, al = split2(a)
    bh, bl = split2(b)
    return dot_nn(jnp.concatenate([ah, al, ah], 1), jnp.concatenate([bh, bh, bl], 0))

def body(nc, ids, *refs):
    toks = refs[:nc]
    w_ref, wba_ref, dec_ref, gain_ref = refs[nc:nc+4]
    sts = refs[nc+4:2*nc+4]
    wout_ref = refs[2*nc+4]
    out_ref = refs[2*nc+5]
    rows = nc*SPAN
    x = jnp.concatenate([t[...] for t in toks], 0) if nc > 1 else toks[0][...]
    ba = dot_nn(x, wba_ref[...])
    strength = jax.nn.sigmoid(ba)
    soft = jnp.maximum(ba, 0.0) + jnp.log1p(jnp.exp(-jnp.abs(ba)))
    ld = -dec_ref[...] * soft
    ri = lax.broadcasted_iota(jnp.int32, (rows, rows), 0)
    ci = lax.broadcasted_iota(jnp.int32, (rows, rows), 1)
    tri = jnp.where((ri >= ci) & (ri // SPAN == ci // SPAN), 1.0, 0.0).astype(BF)
    l0, rest = ld.astype(BF), None
    rest = ld - l0.astype(F32)
    l1 = rest.astype(BF)
    l2 = (rest - l1.astype(F32)).astype(BF)
    cum = dot_nn(tri, l0) + dot_nn(tri, l1) + dot_nn(tri, l2)
    i2 = lax.broadcasted_iota(jnp.int32, (128, 128), 0)
    j2 = lax.broadcasted_iota(jnp.int32, (128, 128), 1)
    same = i2 // SPAN == j2 // SPAN
    incl = same & (i2 >= j2)
    strict = same & (i2 > j2)
    eye = jnp.where(i2 == j2, 1.0, 0.0).astype(F32)
    gated = []
    for g in range(2):
        blk = dot_nn(x, w_ref[:, g*768:(g+1)*768])
        q = blk[:, :128]
        k = blk[:, 128:256]
        q = q * lax.rsqrt(jnp.sum(q*q, axis=1, keepdims=True) + 1e-6) * DK**-0.5
        k = k * lax.rsqrt(jnp.sum(k*k, axis=1, keepdims=True) + 1e-6)
        tiles = []
        for n in range(nc):
            sl = slice(n*SPAN, (n+1)*SPAN)
            qh, ql = split2(q[sl]); kh, kl = split2(k[sl])
            kk = jnp.concatenate([kh, kh, kl], 1)
            qq3 = jnp.concatenate([qh, ql, qh], 1)
            kk3 = jnp.concatenate([kh, kl, kh], 1)
            gram = dot_nt(jnp.concatenate([qq3, qq3, kk3, kk3], 0), jnp.concatenate([kk, kk], 0))
            two = lambda a, c: jnp.concatenate([a[sl, c:c+1], a[sl, c+1:c+2]], 0)
            beta = two(strength, 4*g)
            gc = two(cum, 4*g+2)
            gm = jnp.broadcast_to(gc, (128, 128))
            dec = jnp.exp(jnp.where(incl, gm - gm.T, 0.0))
            amat = jnp.where(strict, beta * dec * gram[128:], 0.0)
            mmat = jnp.where(incl, dec * gram[:128], 0.0)
            sqk = jnp.concatenate([jnp.concatenate([qh, ql], 1), jnp.concatenate([kh, kl], 1)], 0)
            v2 = jnp.concatenate([blk[sl, 256:384], blk[sl, 384:512]], 0)
            z2 = jnp.concatenate([blk[sl, 512:640], blk[sl, 640:768]], 0)
            tiles.append([amat, mmat, beta, jnp.exp(gc), sqk, v2, z2, n])
        invs = [eye - jnp.where(i2 // 2 == j2 // 2, t[0], 0.0) for t in tiles]
        s = 2
        while s < SPAN:
            mask = (i2 // (2*s) == j2 // (2*s)) & ((i2 // s) % 2 == 1) & ((j2 // s) % 2 == 0)
            es = [mm3(jnp.where(mask, t[0], 0.0), d) for t, d in zip(tiles, invs)]
            invs = [d - mm3(d, e) for d, e in zip(invs, es)]
            s *= 2
        outs = []
        for t, d in zip(tiles, invs):
            amat, mmat, beta, eg, sqk, v2, z2, n = t
            st = jnp.concatenate([sts[n][0, 2*g], sts[n][0, 2*g+1]], 1)
            sp = dot_nn(sqk, jnp.concatenate([st, st], 0))
            pair = lambda a: jnp.concatenate([a[:, :128], a[:, 128:]], 0)
            r2 = beta * (v2 - eg * pair(sp[SPAN:]))
            u2 = mm3(d, r2)
            o2 = eg * pair(sp[:SPAN]) + mm3(mmat, u2)
            o2 = o2 * lax.rsqrt(jnp.mean(o2*o2, axis=1, keepdims=True) + 1e-6)
            o2 = o2 * gain_ref[...] * (z2 * jax.nn.sigmoid(z2))
            outs.append(o2.astype(BF))
        for j in range(2):
            gated.append(jnp.concatenate([o[j*SPAN:(j+1)*SPAN] for o in outs], 0) if nc > 1 else outs[0][j*SPAN:(j+1)*SPAN])
    gt = jnp.concatenate(gated, 1)
    for c in range(0, 2048, 512):
        out_ref[:, c:c+512] = dot_nn(gt, wout_ref[:, c:c+512]).astype(BF)

def delta_call(ids, tokens, w, wba, dec, gain, states, wout, nc, steps, vmem=60*2**20):
    specs = [pl.BlockSpec((SPAN, 2048), lambda i, ids, c=c: (ids[i*nc+c], 0)) for c in range(nc)]
    specs += [pl.BlockSpec((2048, 1536), lambda i, ids: (0, 0)), pl.BlockSpec((2048, 128), lambda i, ids: (0, 0)),
              pl.BlockSpec((1, 128), lambda i, ids: (0, 0)), pl.BlockSpec((1, 128), lambda i, ids: (0, 0))]
    specs += [pl.BlockSpec((1, 4, 128, 128), lambda i, ids, c=c: (ids[steps*nc+i*nc+c], 0, 0, 0)) for c in range(nc)]
    specs += [pl.BlockSpec((512, 2048), lambda i, ids: (0, 0))]
    return pl.pallas_call(
        functools.partial(body, nc),
        grid_spec=pltpu.PrefetchScalarGridSpec(num_scalar_prefetch=1, grid=(steps,), in_specs=specs,
            out_specs=pl.BlockSpec((nc*SPAN, 2048), lambda i, ids: (i, 0))),
        out_shape=jax.ShapeDtypeStruct((steps*nc*SPAN, 2048), BF),
        compiler_params=pltpu.CompilerParams(vmem_limit_bytes=vmem),
    )(ids, *([tokens]*nc), w, wba, dec, gain, *([states]*nc), wout)


from jax.sharding import PartitionSpec as P

CHILD_DEV = 8


def gate_lanes(decay_rate, w_ba):
    heads = decay_rate.shape[0]
    lanes = jnp.zeros((1, 128), F32)
    for h in range(heads):
        lanes = lanes.at[0, 4 * (h // 2) + 2 + h % 2].set(decay_rate[h])
    return lanes, jnp.pad(w_ba, ((0, 0), (0, 128 - w_ba.shape[1])))


def shards(tokens, parent_state, parent_index, w_qkvz, w_ba, decay_rate, norm_gain, w_out):
    my_rep = lax.axis_index("rep")
    mine = lax.dynamic_slice_in_dim(parent_index, my_rep * CHILD_DEV, CHILD_DEV)
    rows = lax.all_gather(tokens, "head", axis=0, tiled=True)
    states = lax.all_gather(parent_state, "rep", axis=0, tiled=True)
    lanes, wba = gate_lanes(decay_rate, w_ba)
    ids = jnp.concatenate([jnp.arange(CHILD_DEV, dtype=jnp.int32), mine])
    part = delta_call(ids, rows, w_qkvz, wba, lanes, norm_gain[None], states, w_out, 4, 2)
    return lax.psum_scatter(part, "head", scatter_dimension=0, tiled=True)


def solution(mesh):
    in_specs = (
        P(("rep", "head"), None),
        P("rep", "head", None, None),
        P(),
        P(None, "head"),
        P(None, "head"),
        P("head"),
        P(),
        P("head", None),
    )
    out_specs = P(("rep", "head"), None)
    return jax.shard_map(shards, mesh=mesh, in_specs=in_specs, out_specs=out_specs, check_vma=False)
```

```python
import functools

import jax
import jax.numpy as jnp
from jax import lax
from jax.experimental import pallas as pl
from jax.experimental.pallas import tpu as pltpu
from jax.sharding import PartitionSpec as P

DK = 128
SPAN = 64
CHILDREN = 8
BF = jnp.bfloat16
F32 = jnp.float32


def split2(a):
    hi = a.astype(BF)
    return hi, (a - hi.astype(F32)).astype(BF)


def dot_nn(a, b):
    return lax.dot_general(a, b, (((1,), (0,)), ((), ())), preferred_element_type=F32)


def dot_nt(a, b):
    return lax.dot_general(a, b, (((1,), (1,)), ((), ())), preferred_element_type=F32)


def mm3(a, b):
    ah, al = split2(a)
    bh, bl = split2(b)
    return dot_nn(jnp.concatenate([ah, al, ah], 1), jnp.concatenate([bh, bh, bl], 0))


def small_inverse(a, i8):
    blocks = []
    lane = lax.broadcasted_iota(jnp.int32, (8, 128), 1)
    for b in range(16):
        base = 8 * b
        part = a[base : base + 8]
        t = jnp.where(lane == i8 + base, 1.0, 0.0).astype(F32)
        for r in range(7):
            col = jnp.where(i8[:, :1] > r, part[:, base + r : base + r + 1], 0.0)
            t = t - col * t[r : r + 1]
        blocks.append(t)
    return jnp.concatenate(blocks, 0)


def prep_body(parts, *refs):
    nc = len(parts)
    tok_refs = refs[: sum(parts)]
    w_ref, wba_ref, dec_ref, gain_ref = refs[sum(parts) : sum(parts) + 4]
    outs = refs[sum(parts) + 4 :]
    rows = nc * SPAN
    rows_x = []
    at = 0
    for p in parts:
        rows_x.append(tok_refs[at][...] if p == 1 else jnp.concatenate([t[...] for t in tok_refs[at : at + p]], 1))
        at += p
    x = jnp.concatenate(rows_x, 0) if nc > 1 else rows_x[0]
    ba = dot_nn(x, wba_ref[...])
    strength = jax.nn.sigmoid(ba)
    soft = jnp.maximum(ba, 0.0) + jnp.log1p(jnp.exp(-jnp.abs(ba)))
    ld = -dec_ref[...] * soft
    ri = lax.broadcasted_iota(jnp.int32, (rows, rows), 0)
    ci = lax.broadcasted_iota(jnp.int32, (rows, rows), 1)
    tri = jnp.where((ri >= ci) & (ri // SPAN == ci // SPAN), 1.0, 0.0).astype(BF)
    l0 = ld.astype(BF)
    left = ld - l0.astype(F32)
    l1 = left.astype(BF)
    l2 = (left - l1.astype(F32)).astype(BF)
    cum = dot_nn(tri, l0) + dot_nn(tri, l1) + dot_nn(tri, l2)
    i2 = lax.broadcasted_iota(jnp.int32, (128, 128), 0)
    j2 = lax.broadcasted_iota(jnp.int32, (128, 128), 1)
    i8 = lax.broadcasted_iota(jnp.int32, (8, 128), 0)
    same = i2 // SPAN == j2 // SPAN
    incl = same & (i2 >= j2)
    strict = same & (i2 > j2)
    tiles = []
    for g in range(2):
        blk = dot_nn(x, w_ref[:, g * 768 : (g + 1) * 768])
        q = blk[:, :128]
        k = blk[:, 128:256]
        q = q * lax.rsqrt(jnp.sum(q * q, axis=1, keepdims=True) + 1e-6) * DK**-0.5
        k = k * lax.rsqrt(jnp.sum(k * k, axis=1, keepdims=True) + 1e-6)
        for n in range(nc):
            sl = slice(n * SPAN, (n + 1) * SPAN)
            qh, ql = split2(q[sl])
            kh, kl = split2(k[sl])
            kk = jnp.concatenate([kh, kh, kl], 1)
            qq3 = jnp.concatenate([qh, ql, qh], 1)
            kk3 = jnp.concatenate([kh, kl, kh], 1)
            gram = dot_nt(jnp.concatenate([qq3, qq3, kk3, kk3], 0), jnp.concatenate([kk, kk], 0))

            def two(a, c):
                return jnp.concatenate([a[sl, c : c + 1], a[sl, c + 1 : c + 2]], 0)

            beta = two(strength, 4 * g)
            gc = two(cum, 4 * g + 2)
            gm = jnp.broadcast_to(gc, (128, 128))
            dec = jnp.exp(jnp.where(incl, gm - gm.T, 0.0))
            amat = jnp.where(strict, beta * dec * gram[128:], 0.0)
            mmat = jnp.where(incl, dec * gram[:128], 0.0)
            eg = jnp.exp(gc)
            q2 = jnp.concatenate([q[sl], q[sl]], 0)
            k2 = jnp.concatenate([k[sl], k[sl]], 0)
            v2 = jnp.concatenate([blk[sl, 256:384], blk[sl, 384:512]], 0)
            z2 = jnp.concatenate([blk[sl, 512:640], blk[sl, 640:768]], 0)
            gate = gain_ref[...] * (z2 * jax.nn.sigmoid(z2))
            outs[3 * n + 2][g * 128 : (g + 1) * 128] = gate
            tiles.append([amat, mmat, jnp.concatenate([beta * eg * k2, beta * v2], 1), eg * q2, n, g])
    invs = [small_inverse(t[0], i8) for t in tiles]
    s = 8
    while s < SPAN:
        mask = (i2 // (2 * s) == j2 // (2 * s)) & ((i2 // s) % 2 == 1) & ((j2 // s) % 2 == 0)
        es = [mm3(jnp.where(mask, t[0], 0.0), d) for t, d in zip(tiles, invs)]
        invs = [d - mm3(d, e) for d, e in zip(invs, es)]
        s *= 2
    wus = [mm3(d, t[2]) for t, d in zip(tiles, invs)]
    xys = [mm3(t[1], wu) for t, wu in zip(tiles, wus)]
    for t, xy in zip(tiles, xys):
        n, g = t[4], t[5]
        xh, xl = split2(t[3] - xy[:, :128])
        outs[3 * n][g * 128 : (g + 1) * 128] = jnp.concatenate([xh, xl], 1)
        outs[3 * n + 1][g * 128 : (g + 1) * 128] = xy[:, 128:]


def prep_call(children, w, wba, dec, gain):
    parts = [len(c) for c in children]
    pieces = [p for c in children for p in c]
    full = pl.BlockSpec(memory_space=pltpu.VMEM)
    shapes = [
        jax.ShapeDtypeStruct((256, 256), BF),
        jax.ShapeDtypeStruct((256, 128), F32),
        jax.ShapeDtypeStruct((256, 128), F32),
    ]
    out = pl.pallas_call(
        functools.partial(prep_body, parts),
        in_specs=[full] * (len(pieces) + 4),
        out_specs=[full] * (3 * len(parts)),
        out_shape=shapes * len(parts),
        compiler_params=pltpu.CompilerParams(vmem_limit_bytes=VMEM_KERNEL),
        cost_estimate=pl.CostEstimate(flops=4 * 10**9, bytes_accessed=7 * 2**20, transcendentals=0),
    )(*pieces, w, wba, dec, gain)
    return [out[3 * n : 3 * n + 3] for n in range(len(parts))]


def apply_body(nc, halves, table, *refs):
    ready = refs[: 3 * nc]
    wout_ref, own0, own1, far0, far1, whole_ref = refs[3 * nc : 3 * nc + 6]
    outs = refs[3 * nc + 6 :]
    core, fits = table[4], table[5]
    rows = []
    for n in range(nc):
        child = table[n]
        x_ref, y_ref, g_ref = ready[3 * n : 3 * n + 3]
        heads = []
        for h in range(4):
            own, far = (own0, far0) if h % 2 == 0 else (own1, far1)
            st = jnp.where(core == h // 2, own[child], far[child])
            st = jnp.where(fits == 1, st, whole_ref[child, h])
            sl = slice(h * SPAN, (h + 1) * SPAN)
            o = dot_nn(x_ref[sl], jnp.concatenate([st, st], 0)) + y_ref[sl]
            o = o * lax.rsqrt(jnp.mean(o * o, axis=1, keepdims=True) + 1e-6)
            heads.append((o * g_ref[sl]).astype(BF))
        rows.append(jnp.concatenate(heads, 1))
    gt = jnp.concatenate(rows, 0) if nc > 1 else rows[0]
    for c in range(0, 2048, 512):
        y = dot_nn(gt, wout_ref[:, c : c + 512]).astype(BF)
        if halves:
            outs[c // 1024][:, c % 1024 : c % 1024 + 512] = y
        else:
            for n in range(nc):
                outs[n][:, c : c + 512] = y[n * SPAN : (n + 1) * SPAN]


def apply_call(table, ready, wout, states, halves=False):
    full = pl.BlockSpec(memory_space=pltpu.VMEM)
    nc = len(ready)
    shape = (SPAN, 1024) if halves else (SPAN, 2048)
    n_out = 2 if halves else nc
    return pl.pallas_call(
        functools.partial(apply_body, nc, halves),
        grid_spec=pltpu.PrefetchScalarGridSpec(
            num_scalar_prefetch=1,
            grid=(),
            in_specs=[full] * (3 * nc + 6),
            out_specs=[full] * n_out,
        ),
        out_shape=[jax.ShapeDtypeStruct(shape, BF)] * n_out,
        compiler_params=pltpu.CompilerParams(vmem_limit_bytes=12 * 2**20),
        cost_estimate=pl.CostEstimate(flops=2 * 10**9, bytes_accessed=3 * 2**20, transcendentals=0),
    )(table, *[a for r in ready for a in r], wout, *states)


VMEM_KERNEL = 24 * 2**20
SLOTS = 3


def pick_body(n_in, per_in, counts, sel, *refs):
    bufs, outs = refs[:n_in], refs[n_in:]
    at = 0
    for k, count in enumerate(counts):
        for s in range(count):
            code = sel[at]
            at += 1
            for y in range(n_in):
                @pl.when(code // per_in == y)
                def _():
                    outs[k][s] = bufs[y][code % per_in]


def pick_call(sel, bufs, counts):
    full = pl.BlockSpec(memory_space=pltpu.VMEM)
    return pl.pallas_call(
        functools.partial(pick_body, len(bufs), bufs[0].shape[0], counts),
        grid_spec=pltpu.PrefetchScalarGridSpec(
            num_scalar_prefetch=1,
            grid=(),
            in_specs=[full] * len(bufs),
            out_specs=[full] * len(counts),
        ),
        out_shape=[jax.ShapeDtypeStruct((n,) + bufs[0].shape[1:], BF) for n in counts],
        cost_estimate=pl.CostEstimate(flops=0, bytes_accessed=2**20, transcendentals=0),
        compiler_params=pltpu.CompilerParams(vmem_limit_bytes=8 * 2**20),
    )(sel, *bufs)


def rep_shift(dy, dx, dc):
    pairs = []
    for y in range(4):
        for x in range(4):
            for c in range(2):
                to = ((y + dy) % 4 * 4 + (x + dx) % 4) * 2 + (c + dc) % 2
                pairs.append(((y * 4 + x) * 2 + c, to))
    return pairs


def along_z(a, step):
    return lax.ppermute(a, "head", [(i, (i + step) % 8) for i in range(8)])


def route_tables(parent_index, rep):
    par = parent_index.reshape(32, CHILDREN)
    column = (par // 8) % 4
    i8 = jnp.arange(CHILDREN)
    same = par[:, :, None] == par[:, None, :]
    before = (i8[None, :] < i8[:, None])[None]
    first = ~jnp.any(same & before, axis=2)
    rank = jnp.sum((column[:, :, None] == column[:, None, :]) & before & first[:, None, :], axis=2)
    slot = jnp.sum(jnp.where(same & first[:, None, :], rank[:, None, :], 0), axis=2)
    fits = jnp.max(slot) < SLOTS
    slot = jnp.minimum(slot, SLOTS - 1)
    y, x, c = rep // 8, (rep // 2) % 4, rep % 2
    code = ((y - par // 32) % 4) * 8 + (((par // 4) % 2 + c) % 2) * 4 + par % 4
    mine = first & (column == x)
    table = jnp.stack([jnp.sum(jnp.where(mine & (slot == s), code, 0), axis=1) for s in range(SLOTS)], axis=1)
    k8 = jnp.arange(8)
    to = y * 8 + ((x + k8 // 2) % 4) * 2 + k8 % 2
    sel = jnp.sum(jnp.where((to[:, None] == jnp.arange(32)[None, :])[:, :, None], table[None], 0), axis=1)
    sel = jnp.minimum(sel, 31).reshape(8 * SLOTS)
    arrive = ((x - column) % 4) * (2 * SLOTS) + (jnp.arange(32)[:, None] % 2) * SLOTS + slot
    mate = rep + 1 - 2 * c
    two = jnp.stack([rep, mate])
    here = jnp.sum(jnp.where((two[:, None] == jnp.arange(32)[None, :])[:, :, None], arrive[None], 0), axis=1)
    own = lax.dynamic_slice_in_dim(par, rep, 1)[0]
    return fits, sel.astype(jnp.int32), here.reshape(16).astype(jnp.int32), own


def gate_lanes(decay_rate, w_ba):
    lane = jnp.arange(128)
    head = lane // 4 * 2 + lane % 2
    valid = (lane < 8) & (lane % 4 >= 2)
    spread = jnp.where(valid[None] & (head[None] == jnp.arange(4)[:, None]), decay_rate[:, None], 0.0)
    return jnp.sum(spread, axis=0, keepdims=True), jnp.pad(w_ba, ((0, 0), (0, 128 - w_ba.shape[1])))


def add(a, b):
    return (a.astype(F32) + b.astype(F32)).astype(BF)


def add_half(a, half, right):
    wide = a.astype(F32)
    if right:
        out = jnp.concatenate([wide[:, :1024] + half.astype(F32), wide[:, 1024:]], 1)
    else:
        out = jnp.concatenate([wide[:, :1024], wide[:, 1024:] + half.astype(F32)], 1)
    return out.astype(BF)


def shards(tokens, parent_state, parent_index, w_qkvz, w_ba, decay_rate, norm_gain, w_out):
    rep = lax.axis_index("rep")
    z = lax.axis_index("head")
    core = rep % 2
    lanes, wba = gate_lanes(decay_rate, w_ba)

    def prep(*children):
        return prep_call(children, w_qkvz, wba, lanes, norm_gain[None])

    def mate(a):
        return lax.ppermute(a, "rep", rep_shift(0, 0, 1))

    keep = lax.dynamic_slice_in_dim(parent_state, 2 * core, 2, axis=1)
    other = mate(lax.dynamic_slice_in_dim(parent_state, 2 - 2 * core, 2, axis=1))
    chip = jnp.concatenate([keep, other], 0)
    column = [chip] + [lax.ppermute(chip, "rep", rep_shift(dy, 0, 0)) for dy in (1, 2, 3)]
    fits, sel, here, mine = route_tables(parent_index, rep)

    def whole():
        copies = jnp.broadcast_to(parent_state[None], (32,) + parent_state.shape)
        everyone = lax.all_to_all(copies, "rep", 0, 0).reshape((-1,) + parent_state.shape[1:])
        return jnp.take(everyone, mine, axis=0)

    spare = lax.cond(fits, lambda: jnp.zeros((CHILDREN,) + parent_state.shape[1:], BF), whole)
    sel, spare = lax.optimization_barrier((sel, spare))
    picked = pick_call(sel, column, [2 * SLOTS] * 4)
    came = [picked[0]] + [lax.ppermute(picked[dx], "rep", rep_shift(0, dx, 0)) for dx in (1, 2, 3)]
    own, send = pick_call(here, came, [CHILDREN] * 2)
    far = mate(send)
    states = [own[:, 0], own[:, 1], far[:, 0], far[:, 1], spare]
    flags = jnp.stack([core, fits.astype(jnp.int32)])

    r1, l1 = along_z(tokens, 1), along_z(tokens, -1)
    r2, l2 = along_z(r1, 1), along_z(l1, -1)
    r3, l3 = along_z(r2, 1), along_z(l2, -1)
    r4, l4 = along_z(r3[:, :1024], 1), along_z(l3[:, 1024:], -1)
    ready = {}
    ready[0], ready[1], ready[7] = prep([tokens], [l1], [r1])
    ready[2], ready[6] = prep([l2], [r2])
    ready[3], ready[5] = prep([l3], [r3])
    (ready[4],) = prep([r4, l4])

    def run(offsets, split=False, after=()):
        child = [(z + o) % 8 for o in offsets] + [0] * (4 - len(offsets))
        ids = jnp.concatenate([jnp.stack(child).astype(jnp.int32), flags])
        ids, _ = lax.optimization_barrier((ids, after))
        return apply_call(ids, [ready[o] for o in offsets], w_out, states, split)

    r, l = run([4], True)
    r, l = along_z(r, 1), along_z(l, -1)
    pr, pl_ = run([3, 5])
    sr, sl = add_half(pr, r, True), add_half(pl_, l, False)
    r, l = along_z(sr, 1), along_z(sl, -1)
    pr, pl_ = run([2, 6], after=(sr, sl))
    sr, sl = add(pr, r), add(pl_, l)
    r, l = along_z(sr, 1), along_z(sl, -1)
    pr, pl_, me = run([1, 7, 0], after=(sr, sl))
    sr, sl = add(pr, r), add(pl_, l)
    r, l = along_z(sr, 1), along_z(sl, -1)
    return (r.astype(F32) + l.astype(F32) + me.astype(F32)).astype(BF)


def solution(mesh):
    in_specs = (
        P(("rep", "head"), None),
        P("rep", "head", None, None),
        P(),
        P(None, "head"),
        P(None, "head"),
        P("head"),
        P(),
        P("head", None),
    )
    out_specs = P(("rep", "head"), None)
    return jax.shard_map(shards, mesh=mesh, in_specs=in_specs, out_specs=out_specs, check_vma=False)
```

```python
import functools

import jax
import jax.numpy as jnp
from jax import lax
from jax.experimental import pallas as pl
from jax.experimental.pallas import tpu as pltpu
from jax.sharding import PartitionSpec as P

DK = 128
SPAN = 64
CHILDREN = 8
BF = jnp.bfloat16
F32 = jnp.float32


def split2(a):
    hi = a.astype(BF)
    return hi, (a - hi.astype(F32)).astype(BF)


def dot_nn(a, b):
    return lax.dot_general(a, b, (((1,), (0,)), ((), ())), preferred_element_type=F32)


def dot_nt(a, b):
    return lax.dot_general(a, b, (((1,), (1,)), ((), ())), preferred_element_type=F32)


def mm3(a, b):
    ah, al = split2(a)
    bh, bl = split2(b)
    return dot_nn(jnp.concatenate([ah, al, ah], 1), jnp.concatenate([bh, bh, bl], 0))


def small_inverse(a, i8):
    blocks = []
    lane = lax.broadcasted_iota(jnp.int32, (8, 128), 1)
    for b in range(16):
        base = 8 * b
        part = a[base : base + 8]
        t = jnp.where(lane == i8 + base, 1.0, 0.0).astype(F32)
        for r in range(7):
            col = jnp.where(i8[:, :1] > r, part[:, base + r : base + r + 1], 0.0)
            t = t - col * t[r : r + 1]
        blocks.append(t)
    return jnp.concatenate(blocks, 0)


def prep_body(parts, *refs):
    nc = len(parts)
    tok_refs = refs[: sum(parts)]
    w_ref, wba_ref, dec_ref, gain_ref = refs[sum(parts) : sum(parts) + 4]
    outs = refs[sum(parts) + 4 :]
    rows = nc * SPAN
    rows_x = []
    at = 0
    for p in parts:
        rows_x.append(tok_refs[at][...] if p == 1 else jnp.concatenate([t[...] for t in tok_refs[at : at + p]], 1))
        at += p
    x = jnp.concatenate(rows_x, 0) if nc > 1 else rows_x[0]
    ba = dot_nn(x, wba_ref[...])
    strength = jax.nn.sigmoid(ba)
    soft = jnp.maximum(ba, 0.0) + jnp.log1p(jnp.exp(-jnp.abs(ba)))
    ld = -dec_ref[...] * soft
    ri = lax.broadcasted_iota(jnp.int32, (rows, rows), 0)
    ci = lax.broadcasted_iota(jnp.int32, (rows, rows), 1)
    tri = jnp.where((ri >= ci) & (ri // SPAN == ci // SPAN), 1.0, 0.0).astype(BF)
    l0 = ld.astype(BF)
    left = ld - l0.astype(F32)
    l1 = left.astype(BF)
    l2 = (left - l1.astype(F32)).astype(BF)
    cum = dot_nn(tri, l0) + dot_nn(tri, l1) + dot_nn(tri, l2)
    i2 = lax.broadcasted_iota(jnp.int32, (128, 128), 0)
    j2 = lax.broadcasted_iota(jnp.int32, (128, 128), 1)
    i8 = lax.broadcasted_iota(jnp.int32, (8, 128), 0)
    same = i2 // SPAN == j2 // SPAN
    incl = same & (i2 >= j2)
    strict = same & (i2 > j2)
    tiles = []
    for g in range(2):
        blk = dot_nn(x, w_ref[:, g * 768 : (g + 1) * 768])
        q = blk[:, :128]
        k = blk[:, 128:256]
        q = q * lax.rsqrt(jnp.sum(q * q, axis=1, keepdims=True) + 1e-6) * DK**-0.5
        k = k * lax.rsqrt(jnp.sum(k * k, axis=1, keepdims=True) + 1e-6)
        for n in range(nc):
            sl = slice(n * SPAN, (n + 1) * SPAN)
            qh, ql = split2(q[sl])
            kh, kl = split2(k[sl])
            kk = jnp.concatenate([kh, kh, kl], 1)
            qq3 = jnp.concatenate([qh, ql, qh], 1)
            kk3 = jnp.concatenate([kh, kl, kh], 1)
            gram = dot_nt(jnp.concatenate([qq3, qq3, kk3, kk3], 0), jnp.concatenate([kk, kk], 0))

            def two(a, c):
                return jnp.concatenate([a[sl, c : c + 1], a[sl, c + 1 : c + 2]], 0)

            beta = two(strength, 4 * g)
            gc = two(cum, 4 * g + 2)
            gm = jnp.broadcast_to(gc, (128, 128))
            dec = jnp.exp(jnp.where(incl, gm - gm.T, 0.0))
            amat = jnp.where(strict, beta * dec * gram[128:], 0.0)
            mmat = jnp.where(incl, dec * gram[:128], 0.0)
            eg = jnp.exp(gc)
            q2 = jnp.concatenate([q[sl], q[sl]], 0)
            k2 = jnp.concatenate([k[sl], k[sl]], 0)
            v2 = jnp.concatenate([blk[sl, 256:384], blk[sl, 384:512]], 0)
            z2 = jnp.concatenate([blk[sl, 512:640], blk[sl, 640:768]], 0)
            gate = gain_ref[...] * (z2 * jax.nn.sigmoid(z2))
            outs[3 * n + 2][g * 128 : (g + 1) * 128] = gate
            tiles.append([amat, mmat, jnp.concatenate([beta * eg * k2, beta * v2], 1), eg * q2, n, g])
    invs = [small_inverse(t[0], i8) for t in tiles]
    s = 8
    while s < SPAN:
        mask = (i2 // (2 * s) == j2 // (2 * s)) & ((i2 // s) % 2 == 1) & ((j2 // s) % 2 == 0)
        es = [mm3(jnp.where(mask, t[0], 0.0), d) for t, d in zip(tiles, invs)]
        invs = [d - mm3(d, e) for d, e in zip(invs, es)]
        s *= 2
    wus = [mm3(d, t[2]) for t, d in zip(tiles, invs)]
    xys = [mm3(t[1], wu) for t, wu in zip(tiles, wus)]
    for t, xy in zip(tiles, xys):
        n, g = t[4], t[5]
        xh, xl = split2(t[3] - xy[:, :128])
        outs[3 * n][g * 128 : (g + 1) * 128] = jnp.concatenate([xh, xl], 1)
        outs[3 * n + 1][g * 128 : (g + 1) * 128] = xy[:, 128:]


def prep_call(children, w, wba, dec, gain):
    parts = [len(c) for c in children]
    pieces = [p for c in children for p in c]
    full = pl.BlockSpec(memory_space=pltpu.VMEM)
    shapes = [
        jax.ShapeDtypeStruct((256, 256), BF),
        jax.ShapeDtypeStruct((256, 128), F32),
        jax.ShapeDtypeStruct((256, 128), F32),
    ]
    out = pl.pallas_call(
        functools.partial(prep_body, parts),
        in_specs=[full] * (len(pieces) + 4),
        out_specs=[full] * (3 * len(parts)),
        out_shape=shapes * len(parts),
        compiler_params=pltpu.CompilerParams(vmem_limit_bytes=VMEM_KERNEL),
        cost_estimate=pl.CostEstimate(flops=4 * 10**9, bytes_accessed=7 * 2**20, transcendentals=0),
    )(*pieces, w, wba, dec, gain)
    return [out[3 * n : 3 * n + 3] for n in range(len(parts))]


def apply_body(nc, halves, table, *refs):
    ready = refs[: 3 * nc]
    wout_ref, own0, own1, far0, far1, whole_ref = refs[3 * nc : 3 * nc + 6]
    outs = refs[3 * nc + 6 :]
    core, fits = table[4], table[5]
    rows = []
    for n in range(nc):
        child = table[n]
        x_ref, y_ref, g_ref = ready[3 * n : 3 * n + 3]
        heads = []
        for h in range(4):
            own, far = (own0, far0) if h % 2 == 0 else (own1, far1)
            st = jnp.where(core == h // 2, own[child], far[child])
            st = jnp.where(fits == 1, st, whole_ref[child, h])
            sl = slice(h * SPAN, (h + 1) * SPAN)
            o = dot_nn(x_ref[sl], jnp.concatenate([st, st], 0)) + y_ref[sl]
            o = o * lax.rsqrt(jnp.mean(o * o, axis=1, keepdims=True) + 1e-6)
            heads.append((o * g_ref[sl]).astype(BF))
        rows.append(jnp.concatenate(heads, 1))
    gt = jnp.concatenate(rows, 0) if nc > 1 else rows[0]
    for c in range(0, 2048, 512):
        y = dot_nn(gt, wout_ref[:, c : c + 512]).astype(BF)
        if halves:
            outs[c // 1024][:, c % 1024 : c % 1024 + 512] = y
        else:
            for n in range(nc):
                outs[n][:, c : c + 512] = y[n * SPAN : (n + 1) * SPAN]


def apply_call(table, ready, wout, states, halves=False):
    full = pl.BlockSpec(memory_space=pltpu.VMEM)
    nc = len(ready)
    shape = (SPAN, 1024) if halves else (SPAN, 2048)
    n_out = 2 if halves else nc
    return pl.pallas_call(
        functools.partial(apply_body, nc, halves),
        grid_spec=pltpu.PrefetchScalarGridSpec(
            num_scalar_prefetch=1,
            grid=(),
            in_specs=[full] * (3 * nc + 6),
            out_specs=[full] * n_out,
        ),
        out_shape=[jax.ShapeDtypeStruct(shape, BF)] * n_out,
        compiler_params=pltpu.CompilerParams(vmem_limit_bytes=12 * 2**20),
        cost_estimate=pl.CostEstimate(flops=2 * 10**9, bytes_accessed=3 * 2**20, transcendentals=0),
    )(table, *[a for r in ready for a in r], wout, *states)


VMEM_KERNEL = 24 * 2**20
SLOTS = 3


def pick_body(n_in, per_in, counts, sel, *refs):
    bufs, outs = refs[:n_in], refs[n_in:]
    at = 0
    for k, count in enumerate(counts):
        for s in range(count):
            code = sel[at]
            at += 1
            for y in range(n_in):
                @pl.when(code // per_in == y)
                def _():
                    outs[k][s] = bufs[y][code % per_in]


def pick_call(sel, bufs, counts):
    full = pl.BlockSpec(memory_space=pltpu.VMEM)
    return pl.pallas_call(
        functools.partial(pick_body, len(bufs), bufs[0].shape[0], counts),
        grid_spec=pltpu.PrefetchScalarGridSpec(
            num_scalar_prefetch=1,
            grid=(),
            in_specs=[full] * len(bufs),
            out_specs=[full] * len(counts),
        ),
        out_shape=[jax.ShapeDtypeStruct((n,) + bufs[0].shape[1:], BF) for n in counts],
        cost_estimate=pl.CostEstimate(flops=0, bytes_accessed=2**20, transcendentals=0),
        compiler_params=pltpu.CompilerParams(vmem_limit_bytes=8 * 2**20),
    )(sel, *bufs)


def rep_shift(dy, dx, dc):
    pairs = []
    for y in range(4):
        for x in range(4):
            for c in range(2):
                to = ((y + dy) % 4 * 4 + (x + dx) % 4) * 2 + (c + dc) % 2
                pairs.append(((y * 4 + x) * 2 + c, to))
    return pairs


def along_z(a, step):
    return lax.ppermute(a, "head", [(i, (i + step) % 8) for i in range(8)])


def route_tables(parent_index, rep):
    par = parent_index.reshape(32, CHILDREN)
    column = (par // 8) % 4
    i8 = jnp.arange(CHILDREN)
    same = par[:, :, None] == par[:, None, :]
    before = (i8[None, :] < i8[:, None])[None]
    first = ~jnp.any(same & before, axis=2)
    rank = jnp.sum((column[:, :, None] == column[:, None, :]) & before & first[:, None, :], axis=2)
    slot = jnp.sum(jnp.where(same & first[:, None, :], rank[:, None, :], 0), axis=2)
    fits = jnp.max(slot) < SLOTS
    slot = jnp.minimum(slot, SLOTS - 1)
    y, x, c = rep // 8, (rep // 2) % 4, rep % 2
    code = ((y - par // 32) % 4) * 8 + (((par // 4) % 2 + c) % 2) * 4 + par % 4
    mine = first & (column == x)
    table = jnp.stack([jnp.sum(jnp.where(mine & (slot == s), code, 0), axis=1) for s in range(SLOTS)], axis=1)
    k8 = jnp.arange(8)
    to = y * 8 + ((x + k8 // 2) % 4) * 2 + k8 % 2
    sel = jnp.sum(jnp.where((to[:, None] == jnp.arange(32)[None, :])[:, :, None], table[None], 0), axis=1)
    sel = jnp.minimum(sel, 31).reshape(8 * SLOTS)
    arrive = ((x - column) % 4) * (2 * SLOTS) + (jnp.arange(32)[:, None] % 2) * SLOTS + slot
    mate = rep + 1 - 2 * c
    two = jnp.stack([rep, mate])
    here = jnp.sum(jnp.where((two[:, None] == jnp.arange(32)[None, :])[:, :, None], arrive[None], 0), axis=1)
    own = lax.dynamic_slice_in_dim(par, rep, 1)[0]
    return fits, sel.astype(jnp.int32), here.reshape(16).astype(jnp.int32), own


def gate_lanes(decay_rate, w_ba):
    lane = jnp.arange(128)
    head = lane // 4 * 2 + lane % 2
    valid = (lane < 8) & (lane % 4 >= 2)
    spread = jnp.where(valid[None] & (head[None] == jnp.arange(4)[:, None]), decay_rate[:, None], 0.0)
    return jnp.sum(spread, axis=0, keepdims=True), jnp.pad(w_ba, ((0, 0), (0, 128 - w_ba.shape[1])))


def add(a, b):
    return (a.astype(F32) + b.astype(F32)).astype(BF)


def add_half(a, half, right):
    wide = a.astype(F32)
    if right:
        out = jnp.concatenate([wide[:, :1024] + half.astype(F32), wide[:, 1024:]], 1)
    else:
        out = jnp.concatenate([wide[:, :1024], wide[:, 1024:] + half.astype(F32)], 1)
    return out.astype(BF)


def shards(tokens, parent_state, parent_index, w_qkvz, w_ba, decay_rate, norm_gain, w_out):
    rep = lax.axis_index("rep")
    z = lax.axis_index("head")
    core = rep % 2
    lanes, wba = gate_lanes(decay_rate, w_ba)

    def prep(*children):
        return prep_call(children, w_qkvz, wba, lanes, norm_gain[None])

    def mate(a):
        return lax.ppermute(a, "rep", rep_shift(0, 0, 1))

    keep = lax.dynamic_slice_in_dim(parent_state, 2 * core, 2, axis=1)
    other = mate(lax.dynamic_slice_in_dim(parent_state, 2 - 2 * core, 2, axis=1))
    chip = jnp.concatenate([keep, other], 0)
    column = [chip] + [lax.ppermute(chip, "rep", rep_shift(dy, 0, 0)) for dy in (1, 2, 3)]
    fits, sel, here, mine = route_tables(parent_index, rep)

    def whole():
        copies = jnp.broadcast_to(parent_state[None], (32,) + parent_state.shape)
        everyone = lax.all_to_all(copies, "rep", 0, 0).reshape((-1,) + parent_state.shape[1:])
        return jnp.take(everyone, mine, axis=0)

    spare = lax.cond(fits, lambda: jnp.zeros((CHILDREN,) + parent_state.shape[1:], BF), whole)
    sel, spare = lax.optimization_barrier((sel, spare))
    picked = pick_call(sel, column, [2 * SLOTS] * 4)
    came = [picked[0]] + [lax.ppermute(picked[dx], "rep", rep_shift(0, dx, 0)) for dx in (1, 2, 3)]
    own, send = pick_call(here, came, [CHILDREN] * 2)
    far = mate(send)
    states = [own[:, 0], own[:, 1], far[:, 0], far[:, 1], spare]
    flags = jnp.stack([core, fits.astype(jnp.int32)])

    late_tokens, _ = lax.optimization_barrier((tokens, here))
    r1, l1 = along_z(tokens, 1), along_z(late_tokens, -1)
    r2, l2 = along_z(r1, 1), along_z(l1, -1)
    r3, l3 = along_z(r2, 1), along_z(l2, -1)
    r4, l4 = along_z(r3[:, :1024], 1), along_z(l3[:, 1024:], -1)
    ready = {}
    ready[0], ready[1], ready[7] = prep([tokens], [l1], [r1])
    ready[2], ready[6] = prep([l2], [r2])
    ready[3], ready[5] = prep([l3], [r3])
    (ready[4],) = prep([r4, l4])

    def run(offsets, split=False, after=()):
        child = [(z + o) % 8 for o in offsets] + [0] * (4 - len(offsets))
        ids = jnp.concatenate([jnp.stack(child).astype(jnp.int32), flags])
        ids, _ = lax.optimization_barrier((ids, after))
        return apply_call(ids, [ready[o] for o in offsets], w_out, states, split)

    r, l = run([4], True)
    r, l = along_z(r, 1), along_z(l, -1)
    pr, pl_ = run([3, 5])
    sr, sl = add_half(pr, r, True), add_half(pl_, l, False)
    r, l = along_z(sr, 1), along_z(sl, -1)
    pr, pl_ = run([2, 6], after=(sr, sl))
    sr, sl = add(pr, r), add(pl_, l)
    r, l = along_z(sr, 1), along_z(sl, -1)
    pr, pl_, me = run([1, 7, 0], after=(sr, sl))
    sr, sl = add(pr, r), add(pl_, l)
    r, l = along_z(sr, 1), along_z(sl, -1)
    return (r.astype(F32) + l.astype(F32) + me.astype(F32)).astype(BF)


def solution(mesh):
    in_specs = (
        P(("rep", "head"), None),
        P("rep", "head", None, None),
        P(),
        P(None, "head"),
        P(None, "head"),
        P("head"),
        P(),
        P("head", None),
    )
    out_specs = P(("rep", "head"), None)
    return jax.shard_map(shards, mesh=mesh, in_specs=in_specs, out_specs=out_specs, check_vma=False)
```
